128 devices in a mesh: img: 8 (over z, core), txt: 16 (over y, x).
Axes of the slice: x: 4, y: 4, z: 4, core: 2. Of those that a mesh axis runs over, the one named last changes fastest.
Arguments:
- photo_embedding_raw: bfloat16 [16384, 1152], P(('img', 'txt')), may hold values from -4 to 4
- sentence_embedding_raw: bfloat16 [16384, 1152], P(('txt', 'img')), may hold values from -4 to 4
- photo_match_ids: int32 [16384], P(('img', 'txt')), may hold values from 0 to 16383
- sentence_match_ids: int32 [16384], P(('txt', 'img')), may hold values from 0 to 16383
- sharpness_array: float32 [1], replicated, may hold values from 20 to 40
- offset_term_array: float32 [1], replicated, may hold values from -8 to -6
Outputs:
- image_grad: float32 [16384, 1152], P(('img', 'txt'))
- text_grad: float32 [16384, 1152], P(('txt', 'img'))
- loss: float32 [1], replicated
The draws below stay inside these ranges and needn't reach their ends.
All inputs are finite; a program needn't handle non-finite values.
Results may differ from the reference program's by a relative error of at most 0.0054.
Values may be sent and summed in bfloat16 or wider, within the bound.
A program may use at most 64 MiB of HBM per device.

```python
import math
import jax
import jax.numpy as jnp
from jax import lax

D = 1152
ROWS_DEV = 128
BATCH = 16384
N_TXT = 16


def blend(noise, sub_key, reach):
    height = noise.shape[0]
    width = noise.shape[1]
    narrow = width // 8
    shared = jnp.clip(jax.random.normal(sub_key, (height, narrow), jnp.float32), -4.0, 4.0)
    ramp = reach * (jnp.arange(height, dtype=jnp.float32) + 1.0) / height
    scaled = noise * width ** (-0.5)
    leading = scaled[:, :narrow] + ramp[:, None] * shared * narrow ** (-0.5)
    return jnp.concatenate([leading, scaled[:, narrow:]], axis=1)


def draw_photo_embedding_raw(key, part):
    key = jax.random.fold_in(key, 11)
    noise_key, sub_key = jax.random.split(key)
    noise = jnp.clip(jax.random.normal(noise_key, (BATCH, D), jnp.float32), -6.0, 6.0)
    reach = 1.2
    return blend(noise, sub_key, reach).astype(jnp.bfloat16)


def draw_sentence_embedding_raw(key, part):
    key = jax.random.fold_in(key, 23)
    noise_key, sub_key = jax.random.split(key)
    noise = jnp.clip(jax.random.normal(noise_key, (BATCH, D), jnp.float32), -6.0, 6.0)
    reach = 1.2
    return blend(noise, sub_key, reach).astype(jnp.bfloat16)


def set_ends(result, rng, smallest, top_value):
    longest = result.shape.index(max(result.shape))
    spots = []
    for shift in (0, 1):
        where = [jax.random.randint(jax.random.fold_in(rng, axis), (), 0, length) for axis, length in enumerate(result.shape)]
        where[longest] = (where[longest] + shift) % result.shape[longest]
        spots.append(tuple(where))
    return result.at[spots[0]].set(smallest).at[spots[1]].set(top_value)


def setup_inputs(seed: int = 0) -> dict:
    key_list = jax.random.split(jax.random.key(seed), 7)
    return {
        "photo_embedding_raw": draw_photo_embedding_raw(jax.random.fold_in(key_list[6], 71), 0),
        "sentence_embedding_raw": draw_sentence_embedding_raw(jax.random.fold_in(key_list[6], 71), 0),
        "photo_match_ids": set_ends(jax.random.randint(key_list[2], (BATCH,), 0, BATCH), jax.random.fold_in(key_list[2], 1), 0, BATCH - 1).astype(jnp.int32),
        "sentence_match_ids": set_ends(jax.random.randint(key_list[3], (BATCH,), 0, BATCH), jax.random.fold_in(key_list[3], 1), 0, BATCH - 1).astype(jnp.int32),
        "sharpness_array": jnp.clip(jnp.exp(jax.random.uniform(key_list[4], (1,), jnp.float32, math.log(20.0), math.log(40.0))), 20.0, 40.0),
        "offset_term_array": jnp.clip(jax.random.uniform(key_list[5], (1,), jnp.float32, -8.0, -6.0), -8.0, -6.0),
    }


epsilon = 1e-06

def normalize(values):
    wide = values.astype(jnp.float32)
    inverse = lax.rsqrt(lax.optimization_barrier(jnp.sum(wide * wide, axis=-1, keepdims=True)) + epsilon)
    return (wide * inverse, inverse)

def score_block(picture_row_slice, row_ids, text_rows, column_ids, sharpness_multiplier, offset):
    pair_scores = sharpness_multiplier * jnp.dot(picture_row_slice, text_rows.T, preferred_element_type=jnp.float32) + offset
    positive = (row_ids[:, None] == column_ids[None, :]).astype(jnp.float32)
    signed = 2.0 * positive - 1.0
    share = jnp.sum(jax.nn.softplus(-signed * pair_scores))
    pair_coef = (sharpness_multiplier * (jax.nn.sigmoid(pair_scores) - positive)).astype(jnp.bfloat16)
    return (pair_coef, share)

def backward_norm(unit_rows, inverse, direction):
    along = lax.optimization_barrier(jnp.sum(unit_rows * direction, axis=-1, keepdims=True))
    return inverse * (direction - unit_rows * along)

def reference(photo_embedding_raw, sentence_embedding_raw, photo_match_ids, sentence_match_ids, sharpness_array, offset_term_array):
    sharpness_multiplier = sharpness_array[0]
    offset = offset_term_array[0]
    image_unit, image_inverse = normalize(photo_embedding_raw)
    text_unit, text_inverse = normalize(sentence_embedding_raw)
    image_send = image_unit.astype(jnp.bfloat16)
    text_send = text_unit.astype(jnp.bfloat16)
    row_block = ROWS_DEV * N_TXT
    blocks = BATCH // row_block

    def sweep(running, position):
        text_acc, loss_acc = running
        picture_row_slice = lax.dynamic_slice_in_dim(image_send, position * row_block, row_block, 0)
        row_ids = lax.dynamic_slice_in_dim(photo_match_ids, position * row_block, row_block, 0)
        pair_coef, share = score_block(picture_row_slice, row_ids, text_send, sentence_match_ids, sharpness_multiplier, offset)
        image_part = jnp.dot(pair_coef, text_send, preferred_element_type=jnp.float32)
        text_acc = text_acc + jnp.dot(pair_coef.T, picture_row_slice, preferred_element_type=jnp.float32)
        return ((text_acc, loss_acc + share), image_part)
    initial = (jnp.zeros((BATCH, D), jnp.float32), jnp.zeros((), jnp.float32))
    (text_dir, summed_loss_value), picture_segments = lax.scan(sweep, initial, jnp.arange(blocks, dtype=jnp.int32))
    image_dir = picture_segments.reshape(BATCH, D)
    image_grad = backward_norm(image_unit, image_inverse, image_dir)
    text_grad = backward_norm(text_unit, text_inverse, text_dir)
    loss = (summed_loss_value / BATCH).reshape(1)
    return (image_grad, text_grad, loss)
```

```python
import functools

import jax
import jax.numpy as jnp
from jax import lax
from jax.experimental import pallas as pl
from jax.experimental.pallas import tpu as pltpu
from jax.sharding import PartitionSpec as P

MESH = pl.DeviceIdType.MESH
EPSILON = 1e-06
D = 1152
ROWS = 128
BATCH = 16384
F32 = jnp.float32
BF16 = jnp.bfloat16

POS = {(0, 0): 0, (0, 1): 1, (0, 3): 2, (1, 0): 3, (1, 1): 4, (0, 2): 5, (1, 3): 6, (1, 2): 7}
SENDS = {
    "R": [(0, 0, 64, 128), (0, 0, 0, 64), (1, 0, 0, 64), (0, 3, 64, 128), (1, 3, 0, 64)],
    "L": [(0, 0, 64, 128), (0, 0, 0, 64), (1, 0, 0, 64), (0, 1, 0, 64), (1, 1, 64, 128)],
    "V": [(0, 0, 0, 64), (0, 0, 64, 128), (0, 1, 64, 128), (0, 3, 64, 128)],
}
EVENTS = [(k, link) for k in range(5) for link in "RLV" if k < len(SENDS[link])]
INDEX = {event: i for i, event in enumerate(EVENTS)}
BACK = {"R": "L", "L": "R", "V": "V"}
RETURNS = [
    [(4, "R"), (4, "L"), (3, "V")],
    [(3, "R"), (3, "L")],
    [(2, "R"), (2, "L"), (2, "V")],
    [(1, "R"), (1, "L"), (1, "V")],
    [(0, "R"), (0, "L"), (0, "V")],
]
SIDES = "xy"
ROW_TILE = 512
COL_TILE = 256
SLICE = 16


def landing(link, entry):
    pair, offset, first, last = entry
    if link == "R":
        return (pair, (offset + 3) % 4, first, last)
    if link == "L":
        return (pair, (offset + 1) % 4, first, last)
    return (1 - pair, offset, first, last)


def partners():
    i = lax.axis_index("img")
    t = lax.axis_index("txt")
    z, c, y, x = i // 2, i % 2, t // 4, t % 4

    def at(x, y, z, c):
        return (z * 2 + c, y * 4 + x)

    return {
        "xR": at((x + 1) % 4, y, z, c),
        "xL": at((x + 3) % 4, y, z, c),
        "xV": at(x, y, z + 1 - 2 * (z % 2), c),
        "x2": at((x + 2) % 4, y, z, c),
        "yR": at(x, (y + 1) % 4, z, c),
        "yL": at(x, (y + 3) % 4, z, c),
        "yV": at(x, y, 3 - z, c),
        "y2": at(x, (y + 2) % 4, z, c),
        "sib": at(x, y, z, 1 - c),
        "x1": at(x + 1 - 2 * (x % 2), y, z, c),
        "y1": at(x, y + 1 - 2 * (y % 2), z, c),
    }


BARRIER = ("xR", "xL", "xV", "x2", "yR", "yL", "yV", "y2", "sib")
LOSS_STEPS = ("x1", "x2", "y1", "y2", "xV", "yV", "sib")


def normalize(values):
    wide = values.astype(F32)
    inverse = lax.rsqrt(jnp.sum(wide * wide, axis=-1, keepdims=True) + EPSILON)
    return wide * inverse, inverse


def kernel(
    img_raw, txt_raw, img_ids, txt_ids, sharp_ref, offset_ref,
    img_out, txt_out, loss_out,
    images, texts, coef, coef_t, score0, score1, row_ids, col_ids, img_part, txt_part, loss_acc,
    sib_send, sib_recv, back_send, back_recv, idx, idt, loss_send, loss_recv,
    g_ss, g_rs, f_ss, f_rs, b_ss, b_rs, p_ss, p_rs, i_ss, i_rs, l_ss, l_rs,
):
    to = partners()
    sharp = sharp_ref[0]
    offset = offset_ref[0]
    raw = {"x": img_raw, "y": txt_raw}

    def remote(src, dst, send, recv, where):
        return pltpu.make_async_remote_copy(
            src_ref=src, dst_ref=dst, send_sem=send, recv_sem=recv, device_id=to[where], device_id_type=MESH
        )

    pending = []

    def start(copy):
        copy.start()
        pending.append(copy)

    barrier = pltpu.get_barrier_semaphore()
    for name in BARRIER:
        pl.semaphore_signal(barrier, inc=1, device_id=to[name], device_id_type=MESH)
    images[0:ROWS, :] = normalize(img_raw[...])[0].astype(BF16)
    texts[0:ROWS, :] = normalize(txt_raw[...])[0].astype(BF16)
    idx[0, 0, 0] = img_ids[...]
    idt[0, 0] = txt_ids[...]
    pl.semaphore_wait(barrier, len(BARRIER))

    def rows_of(side, entry):
        pair, off, first, last = entry
        pos = POS[(pair, off)]
        if side == "x":
            return images.at[pl.ds(pos * 256 + first, last - first)]
        return texts.at[pl.ds(pos * 128 + first, last - first)]

    gather = {}
    for side in SIDES:
        for event in EVENTS:
            k, link = event
            n = INDEX[event] + (0 if side == "x" else len(EVENTS))
            entry = SENDS[link][k]
            gather[side, event] = remote(
                rows_of(side, entry), rows_of(side, landing(link, entry)), g_ss.at[n], g_rs.at[n], side + link
            )

    forwards = {}

    def forward(entry):
        n = sum(len(copies) for copies in forwards.values())
        pair, off, first, last = entry
        at = POS[(pair, off)] * 256 + first
        copy = remote(
            images.at[pl.ds(at, last - first)], images.at[pl.ds(at + 128, last - first)], f_ss.at[n], f_rs.at[n], "sib"
        )
        start(copy)
        forwards.setdefault(POS[(pair, off)], []).append(copy)

    def send_slot(k):
        for event in EVENTS:
            if event[0] == k:
                for side in SIDES:
                    start(gather[side, event])

    def receive_slot(k):
        for event in EVENTS:
            if event[0] == k:
                for side in SIDES:
                    gather[side, event].wait_recv()
                forward(landing(event[1], SENDS[event[1]][k]))

    def receive_sibling(*positions):
        for pos in positions:
            for copy in forwards[pos]:
                copy.wait_recv()

    send_slot(0)
    send_slot(1)
    id_copies = {}
    for n, (where, slot) in enumerate((("R", 3), ("L", 1), ("2", 2))):
        id_copies["x", n] = remote(idx.at[0, 0, 0], idx.at[0, 0, slot], i_ss.at[n], i_rs.at[n], "x" + where)
        id_copies["y", n] = remote(idt.at[0, 0], idt.at[0, slot], i_ss.at[3 + n], i_rs.at[3 + n], "y" + where)
    id_copies["x", 3] = remote(idx.at[0, 0], idx.at[0, 1], i_ss.at[6], i_rs.at[6], "xV")
    id_copies["y", 3] = remote(idt.at[0], idt.at[1], i_ss.at[7], i_rs.at[7], "yV")
    id_copies["x", 4] = remote(idx.at[0], idx.at[1], i_ss.at[8], i_rs.at[8], "sib")
    for n in range(3):
        for side in SIDES:
            start(id_copies[side, n])
    forward((0, 0, 0, 128))
    for side in SIDES:
        for n in range(3):
            id_copies[side, n].wait_recv()
        start(id_copies[side, 3])
    id_copies["y", 3].wait_recv()
    for (pair, off), pos in POS.items():
        col_ids[:, pos * 128 : pos * 128 + 128] = idt[pair, off]
    id_copies["x", 3].wait_recv()
    start(id_copies["x", 4])
    receive_slot(0)
    send_slot(2)
    id_copies["x", 4].wait_recv()
    for kind in range(2):
        for (pair, off), pos in POS.items():
            at = pos * 256 + kind * 128
            row_ids[at : at + 128, :] = jnp.broadcast_to(idx[kind, pair, off], (128, 128)).T
    receive_slot(1)
    send_slot(3)
    receive_sibling(0, 1)

    loss_acc[...] = jnp.zeros_like(loss_acc)
    scores = (score0, score1)

    def tile(t):
        k = (t + 15) // 16 + (t + 12) // 16 + (t + 7) // 16
        u = t - k * k
        f = (u - k + 8) // 8
        r = k + f * (u - 2 * k)
        c = u + f * (k - u)
        return pl.multiple_of(r * ROW_TILE, ROW_TILE), pl.multiple_of(c * COL_TILE, COL_TILE)

    def product(t, out):
        r, c = tile(t)
        out[...] = lax.dot_general(
            images[pl.ds(r, ROW_TILE), :],
            texts[pl.ds(c, COL_TILE), :],
            (((1,), (1,)), ((), ())),
            preferred_element_type=F32,
        )

    def pointwise(t, scored):
        r, c = tile(t)
        cols = pl.ds(c, COL_TILE)
        ids = col_ids[:, cols]
        total = jnp.zeros((SLICE, COL_TILE), F32)
        for q in range(ROW_TILE // SLICE):
            rows = pl.ds(r + q * SLICE, SLICE)
            block = row_ids[rows, :]
            positive = jnp.concatenate([block, block], axis=1) == ids
            scale = jnp.where(positive, -sharp, sharp)
            shift = jnp.where(positive, -offset, offset)
            grown = jnp.exp(scale * scored[q * SLICE : (q + 1) * SLICE, :] + shift)
            above = 1.0 + grown
            share = grown * pl.reciprocal(above, approx=True)
            coef[rows, cols] = (share * scale).astype(BF16)
            if q % 8 == 0:
                small = grown
                logs = jnp.log(above)
            else:
                small = small + grown
                logs = logs + jnp.log(above)
            if q % 8 == 7:
                total = total + jnp.where(small < 1e-3, small, logs)
        coef_t[cols, pl.ds(r, ROW_TILE)] = coef[pl.ds(r, ROW_TILE), cols].T
        summed = loss_acc[...]
        for a in range(SLICE // 8):
            for b in range(COL_TILE // 128):
                summed = summed + total[a * 8 : a * 8 + 8, b * 128 : b * 128 + 128]
        loss_acc[...] = summed

    product(0, score0)
    receive_sibling(2, 3)

    def two_tiles(h, _):
        t = 2 * h
        product(t + 1, score1)
        pointwise(t, score0)

        product(t + 2, score0)
        pointwise(t + 1, score1)
        return 0

    two_tiles(0, 0)
    receive_slot(2)
    send_slot(4)
    product(3, score1)
    pointwise(2, score0)
    receive_slot(3)
    receive_sibling(4, 5)
    product(4, score0)
    pointwise(3, score1)
    lax.fori_loop(2, 4, two_tiles, 0)
    receive_slot(4)
    receive_sibling(6, 7)
    lax.fori_loop(4, 7, two_tiles, 0)
    product(15, score1)
    pointwise(14, score0)
    pointwise(15, score1)

    loss_copies = []

    def loss_step():
        n = len(loss_copies)
        if n:
            loss_copies[-1].wait_recv()
            total = loss_send[n - 1] + loss_recv[n - 1]
        else:
            total = loss_acc[...]
        if n < len(LOSS_STEPS):
            loss_send[n] = total
            copy = remote(loss_send.at[n], loss_recv.at[n], l_ss.at[n], l_rs.at[n], LOSS_STEPS[n])
            start(copy)
            loss_copies.append(copy)
        else:
            loss_out[0] = jnp.sum(total) / BATCH

    loss_step()

    parts = {"x": img_part, "y": txt_part}
    returns = {}
    for side in SIDES:
        for event in EVENTS:
            k, link = event
            n = INDEX[event] + (0 if side == "x" else len(EVENTS))
            entry = SENDS[link][k]
            at = n * 64
            returns[side, event] = remote(
                back_send.at[pl.ds(at, 64)], back_recv.at[pl.ds(at, 64)], b_ss.at[n], b_rs.at[n], side + BACK[link]
            )
    sibling = []

    def group(g):
        full = jnp.dot(coef[g * 512 : g * 512 + 512, :], texts[...], preferred_element_type=F32)
        for j in range(2):
            at = (2 * g + j) * 128
            sib_send[at : at + 128, :] = full[j * 256 + 128 : j * 256 + 256].astype(BF16)
            img_part[at : at + 128, :] = full[j * 256 : j * 256 + 128]
        copy = remote(
            sib_send.at[pl.ds(g * 256, 256)], sib_recv.at[pl.ds(g * 256, 256)], p_ss.at[g], p_rs.at[g], "sib"
        )
        start(copy)
        txt_part[g * 256 : g * 256 + 256, :] = jnp.dot(
            coef_t[g * 256 : g * 256 + 256, :], images[...], preferred_element_type=F32
        )
        copy.wait_recv()

    taken = set()

    def total_of(side, pair, off, first, last):
        at = POS[(pair, off)] * 128 + first
        value = parts[side][at : at + last - first, :]
        if side == "x":
            value = value + sib_recv[at : at + last - first, :].astype(F32)
        for event in EVENTS:
            k, link = event
            entry = SENDS[link][k]
            if entry == (pair, off, first, last):
                returns[side, event].wait_recv()
                taken.add((side, event))
                n = INDEX[event] + (0 if side == "x" else len(EVENTS))
                value = value + back_recv[n * 64 : n * 64 + 64, :].astype(F32)
        return value

    def send_back(events):
        for event in events:
            for side in SIDES:
                k, link = event
                n = INDEX[event] + (0 if side == "x" else len(EVENTS))
                value = total_of(side, *landing(link, SENDS[link][k]))
                back_send[n * 64 : n * 64 + 64, :] = value.astype(BF16)
                start(returns[side, event])

    group(3)
    send_back(RETURNS[0])
    loss_step()
    group(2)
    send_back(RETURNS[1])
    loss_step()
    group(1)
    loss_step()
    send_back(RETURNS[2])
    group(0)
    loss_step()
    send_back(RETURNS[3])
    loss_step()
    send_back(RETURNS[4])
    loss_step()
    for half in (0, 64):
        for side, out in (("x", img_out), ("y", txt_out)):
            unit, inverse = normalize(raw[side][half : half + 64, :])
            direction = total_of(side, 0, 0, half, half + 64)
            along = jnp.sum(unit * direction, axis=-1, keepdims=True)
            out[half : half + 64, :] = inverse * (direction - unit * along)
    loss_step()
    for copy in pending:
        copy.wait_send()


def on_device(photo, sentence, photo_ids, sentence_ids, sharp, offset):
    vmem = pl.BlockSpec(memory_space=pltpu.VMEM)
    smem = pl.BlockSpec(memory_space=pltpu.SMEM)
    events = 2 * len(EVENTS)
    dma = pltpu.SemaphoreType.DMA
    return pl.pallas_call(
        kernel,
        out_shape=(
            jax.ShapeDtypeStruct((ROWS, D), F32),
            jax.ShapeDtypeStruct((ROWS, D), F32),
            jax.ShapeDtypeStruct((1,), F32),
        ),
        in_specs=[vmem] * 4 + [smem] * 2,
        out_specs=(vmem, vmem, smem),
        scratch_shapes=[
            pltpu.VMEM((2048, D), BF16),
            pltpu.VMEM((1024, D), BF16),
            pltpu.VMEM((2048, 1024), BF16),
            pltpu.VMEM((1024, 2048), BF16),
            pltpu.VMEM((ROW_TILE, COL_TILE), F32),
            pltpu.VMEM((ROW_TILE, COL_TILE), F32),
            pltpu.VMEM((2048, 128), jnp.int32),
            pltpu.VMEM((1, 1024), jnp.int32),
            pltpu.VMEM((1024, D), F32),
            pltpu.VMEM((1024, D), F32),
            pltpu.VMEM((8, 128), F32),
            pltpu.VMEM((1024, D), BF16),
            pltpu.VMEM((1024, D), BF16),
            pltpu.VMEM((events * 64, D), BF16),
            pltpu.VMEM((events * 64, D), BF16),
            pltpu.VMEM((2, 2, 4, 1, 128), jnp.int32),
            pltpu.VMEM((2, 4, 1, 128), jnp.int32),
            pltpu.VMEM((7, 8, 128), F32),
            pltpu.VMEM((7, 8, 128), F32),
            dma((events,)), dma((events,)),
            dma((16,)), dma((16,)),
            dma((events,)), dma((events,)),
            dma((4,)), dma((4,)),
            dma((9,)), dma((9,)),
            dma((7,)), dma((7,)),
        ],
        compiler_params=pltpu.CompilerParams(
            collective_id=0, has_side_effects=True, vmem_limit_bytes=60 << 20
        ),
        cost_estimate=pl.CostEstimate(flops=3 * 2 * 2048 * 1024 * D, bytes_accessed=1 << 21, transcendentals=3 << 21),
        name="pair_loss",
    )(photo, sentence, photo_ids.reshape(1, ROWS), sentence_ids.reshape(1, ROWS), sharp, offset)


def solution(mesh):
    return jax.shard_map(
        on_device,
        mesh=mesh,
        in_specs=(
            P(("img", "txt"), None),
            P(("txt", "img"), None),
            P(("img", "txt")),
            P(("txt", "img")),
            P(),
            P(),
        ),
        out_specs=(P(("img", "txt"), None), P(("txt", "img"), None), P()),
        check_vma=False,
    )
```

```python
import functools

import jax
import jax.numpy as jnp
from jax import lax
from jax.experimental import pallas as pl
from jax.experimental.pallas import tpu as pltpu
from jax.sharding import PartitionSpec as P

MESH = pl.DeviceIdType.MESH
EPSILON = 1e-06
D = 1152
ROWS = 128
BATCH = 16384
F32 = jnp.float32
BF16 = jnp.bfloat16

POS = {(0, 0): 0, (0, 1): 1, (0, 3): 2, (1, 0): 3, (1, 1): 4, (0, 2): 5, (1, 3): 6, (1, 2): 7}
SENDS = {
    "R": [(0, 0, 64, 128), (0, 0, 0, 64), (1, 0, 0, 64), (0, 3, 64, 128), (1, 3, 0, 64)],
    "L": [(0, 0, 64, 128), (0, 0, 0, 64), (1, 0, 0, 64), (0, 1, 0, 64), (1, 1, 64, 128)],
    "V": [(0, 0, 0, 64), (0, 0, 64, 128), (0, 1, 64, 128), (0, 3, 64, 128)],
}
EVENTS = [(k, link) for k in range(5) for link in "RLV" if k < len(SENDS[link])]
INDEX = {event: i for i, event in enumerate(EVENTS)}
BACK = {"R": "L", "L": "R", "V": "V"}
RETURNS = [
    [(4, "R"), (4, "L")],
    [(3, "R"), (3, "L"), (3, "V")],
    [(2, "R"), (2, "L"), (2, "V")],
    [(1, "R"), (1, "L"), (1, "V")],
    [(0, "R"), (0, "L"), (0, "V")],
]
SIDES = "xy"
SLICE = 16


def landing(link, entry):
    pair, offset, first, last = entry
    if link == "R":
        return (pair, (offset + 3) % 4, first, last)
    if link == "L":
        return (pair, (offset + 1) % 4, first, last)
    return (1 - pair, offset, first, last)


def partners():
    i = lax.axis_index("img")
    t = lax.axis_index("txt")
    z, c, y, x = i // 2, i % 2, t // 4, t % 4

    def at(x, y, z, c):
        return (z * 2 + c, y * 4 + x)

    return {
        "xR": at((x + 1) % 4, y, z, c),
        "xL": at((x + 3) % 4, y, z, c),
        "xV": at(x, y, z + 1 - 2 * (z % 2), c),
        "x2": at((x + 2) % 4, y, z, c),
        "xVR": at((x + 1) % 4, y, z + 1 - 2 * (z % 2), c),
        "xVL": at((x + 3) % 4, y, z + 1 - 2 * (z % 2), c),
        "xV2": at((x + 2) % 4, y, z + 1 - 2 * (z % 2), c),
        "yR": at(x, (y + 1) % 4, z, c),
        "yL": at(x, (y + 3) % 4, z, c),
        "yV": at(x, y, 3 - z, c),
        "y2": at(x, (y + 2) % 4, z, c),
        "yVR": at(x, (y + 1) % 4, 3 - z, c),
        "yVL": at(x, (y + 3) % 4, 3 - z, c),
        "yV2": at(x, (y + 2) % 4, 3 - z, c),
        "sib": at(x, y, z, 1 - c),
    }


PLACES = {"R": (0, 3), "L": (0, 1), "2": (0, 2), "V": (1, 0), "VR": (1, 3), "VL": (1, 1), "V2": (1, 2)}
BARRIER = tuple(side + name for side in SIDES for name in PLACES) + ("sib",)
LOSS_STEPS = (("sib",), ("xV",), ("yV",), ("xR", "xL", "x2"), ("yR", "yL", "y2"))


def normalize(values):
    wide = values.astype(F32)
    inverse = lax.rsqrt(jnp.sum(wide * wide, axis=-1, keepdims=True) + EPSILON)
    return wide * inverse, inverse


def kernel(
    img_hbm, txt_hbm, img_ids, txt_ids, sharp_ref, offset_ref,
    img_out, txt_out, loss_out,
    images, texts, coef, coef_t, score0, score1, img_rows, img_lanes, txt_rows, txt_lanes, img_part, txt_part, loss_acc,
    sib_send, sib_recv, back_send, back_recv, idx, idt, loss_held,
    img_raw, txt_raw, in_sem, g_ss, g_rs, f_ss, f_rs, b_ss, b_rs, p_ss, p_rs, i_ss, i_rs, l_ss, l_rs,
):
    to = partners()
    sharp = sharp_ref[0]
    offset = offset_ref[0]
    raw = {"x": img_raw, "y": txt_raw}

    def remote(src, dst, send, recv, where):
        return pltpu.make_async_remote_copy(
            src_ref=src, dst_ref=dst, send_sem=send, recv_sem=recv, device_id=to[where], device_id_type=MESH
        )

    pending = []

    def start(copy):
        copy.start()
        pending.append(copy)

    barrier = pltpu.get_barrier_semaphore()
    for name in BARRIER:
        pl.semaphore_signal(barrier, inc=1, device_id=to[name], device_id_type=MESH)
    img_load = pltpu.make_async_copy(img_hbm, img_raw, in_sem.at[0])
    txt_load = pltpu.make_async_copy(txt_hbm, txt_raw, in_sem.at[1])
    img_load.start()
    txt_load.start()
    img_load.wait()
    images[0:ROWS, :] = normalize(img_raw[...])[0].astype(BF16)
    txt_load.wait()
    texts[0:ROWS, :] = normalize(txt_raw[...])[0].astype(BF16)
    idx[0, 0, 0] = img_ids[...]
    idt[0, 0] = txt_ids[...]
    pl.semaphore_wait(barrier, len(BARRIER))

    def rows_of(side, entry):
        pair, off, first, last = entry
        pos = POS[(pair, off)]
        if side == "x":
            return images.at[pl.ds(pos * 256 + first, last - first)]
        return texts.at[pl.ds(pos * 128 + first, last - first)]

    gather = {}
    for side in SIDES:
        for event in EVENTS:
            k, link = event
            n = INDEX[event] + (0 if side == "x" else len(EVENTS))
            entry = SENDS[link][k]
            gather[side, event] = remote(
                rows_of(side, entry), rows_of(side, landing(link, entry)), g_ss.at[n], g_rs.at[n], side + link
            )

    forwards = {}

    def forward(entry):
        n = sum(len(copies) for copies in forwards.values())
        pair, off, first, last = entry
        at = POS[(pair, off)] * 256 + first
        copy = remote(
            images.at[pl.ds(at, last - first)], images.at[pl.ds(at + 128, last - first)], f_ss.at[n], f_rs.at[n], "sib"
        )
        start(copy)
        forwards.setdefault(POS[(pair, off)], []).append(copy)

    def send_slot(k):
        for event in EVENTS:
            if event[0] == k:
                for side in SIDES:
                    start(gather[side, event])

    def receive_slot(k):
        for event in EVENTS:
            if event[0] == k:
                for side in SIDES:
                    gather[side, event].wait_recv()
                forward(landing(event[1], SENDS[event[1]][k]))

    def receive_sibling(*positions):
        for pos in positions:
            for copy in forwards[pos]:
                copy.wait_recv()

    id_copies = []
    for name, place in PLACES.items():
        for side, ids in (("x", idx.at[0]), ("y", idt)):
            n = len(id_copies)
            id_copies.append(remote(ids.at[0, 0], ids.at[place], i_ss.at[n], i_rs.at[n], side + name))
            start(id_copies[n])
    send_slot(0)
    send_slot(1)
    forward((0, 0, 0, 128))
    for copy in id_copies:
        copy.wait_recv()
    id_forward = remote(idx.at[0], idx.at[1], i_ss.at[14], i_rs.at[14], "sib")
    start(id_forward)
    for (pair, off), pos in POS.items():
        txt_lanes[:, pos * 128 : pos * 128 + 128] = idt[pair, off]
        if pos == 7:
            txt_rows[...] = jnp.broadcast_to(idt[pair, off], (128, 128)).T

    def spread(kind):
        for (pair, off), pos in POS.items():
            at = pos * 256 + kind * 128
            img_lanes[:, at : at + 128] = idx[kind, pair, off]
            img_rows[at : at + 128, :] = jnp.broadcast_to(idx[kind, pair, off], (128, 128)).T

    receive_slot(0)
    send_slot(2)
    spread(0)
    id_forward.wait_recv()
    spread(1)
    receive_slot(1)
    send_slot(3)
    receive_sibling(0, 1)

    sums = []

    def image_group(first, last):
        n = len(sums)
        full = jnp.dot(coef[first * 256 : last * 256, :], texts[...], preferred_element_type=F32)
        for j in range(last - first):
            at = (first + j) * 128
            sib_send[at : at + 128, :] = full[j * 256 + 128 : j * 256 + 256].astype(BF16)
            img_part[at : at + 128, :] = full[j * 256 : j * 256 + 128]
        rows = pl.ds(first * 128, (last - first) * 128)
        sums.append(remote(sib_send.at[rows], sib_recv.at[rows], p_ss.at[n], p_rs.at[n], "sib"))
        start(sums[n])

    def text_group(first, last):
        txt_part[first * 128 : last * 128, :] = jnp.dot(
            coef_t[first * 128 : last * 128, :], images[...], preferred_element_type=F32
        )

    loss_acc[...] = jnp.zeros_like(loss_acc)

    def product(tile, out):
        texts_first, row, height, col, width = tile
        left, right = (texts, images) if texts_first else (images, texts)
        out[0:height, 0:width] = lax.dot_general(
            left[row : row + height, :],
            right[col : col + width, :],
            (((1,), (1,)), ((), ())),
            preferred_element_type=F32,
        )

    def pointwise(tile, scored):
        texts_first, row, height, col, width = tile
        if texts_first:
            out, out_t, lanes, row_ids = coef_t, coef, img_lanes, txt_rows
            row_ids_at = 0
        else:
            out, out_t, lanes, row_ids = coef, coef_t, txt_lanes, img_rows
            row_ids_at = row
        summed = loss_acc[...]
        for left in range(0, width, 512):
            wide = min(512, width - left)
            cols = slice(col + left, col + left + wide)
            ids = lanes[:, cols]
            for q in range(height // SLICE):
                block = row_ids[row_ids_at + q * SLICE : row_ids_at + (q + 1) * SLICE, :]
                positive = jnp.concatenate([block] * (wide // 128), axis=1) == ids
                scale = jnp.where(positive, -sharp, sharp)
                shift = jnp.where(positive, -offset, offset)
                grown = jnp.exp(scale * scored[q * SLICE : (q + 1) * SLICE, left : left + wide] + shift)
                above = 1.0 + grown
                share = grown * pl.reciprocal(above, approx=True)
                out[row + q * SLICE : row + (q + 1) * SLICE, cols] = (share * scale).astype(BF16)
                if q % 8 == 0:
                    small = grown
                    logs = jnp.log(above)
                else:
                    small = small + grown
                    logs = logs + jnp.log(above)
                if q == 7:
                    total = jnp.where(small < 1e-3, small, logs)
                elif q % 8 == 7:
                    total = total + jnp.where(small < 1e-3, small, logs)
            for a in range(0, SLICE, 8):
                for b in range(0, wide, 128):
                    summed = summed + total[a : a + 8, b : b + 128]
        loss_acc[...] = summed
        rows = slice(row, row + height)
        cols = slice(col, col + width)
        out_t[cols, rows] = out[rows, cols].T

    scores = (score0, score1)
    done = []

    def score(*tiles):
        for tile in tiles:
            product(tile, scores[len(done) % 2])
            if done:
                pointwise(done[-1], scores[(len(done) - 1) % 2])
            done.append(tile)

    score((False, 0, 256, 0, 512), (False, 256, 256, 0, 512))
    receive_sibling(2, 3)
    score((False, 512, 256, 0, 512))
    receive_slot(2)
    send_slot(4)
    score((False, 768, 256, 0, 512))
    receive_sibling(4)
    score((False, 1024, 256, 0, 512))
    receive_slot(3)
    score(*((False, at, 256, 512, 384) for at in range(0, 1280, 256)))
    receive_sibling(5, 6)
    for at in (1280, 1536):
        score((False, at, 256, 0, 512), (False, at, 256, 512, 384))
    receive_slot(4)
    score((True, 896, 128, 0, 896), (True, 896, 128, 896, 896))
    receive_sibling(7)
    score((False, 1792, 256, 0, 512), (False, 1792, 256, 512, 512))
    pointwise(done[-1], scores[(len(done) - 1) % 2])
    image_group(7, 8)

    place = {"x": lax.axis_index("txt") % 4, "y": lax.axis_index("txt") // 4}
    loss_copies = []

    def loss_step():
        n = len(loss_copies)
        if n:
            for copy in loss_copies[-1]:
                copy.wait_recv()
            before = LOSS_STEPS[n - 1]
            if len(before) == 1:
                total = loss_held[n - 1, 0] + loss_held[n - 1, 1]
            else:
                total = (loss_held[n - 1, 0] + loss_held[n - 1, 1]) + (loss_held[n - 1, 2] + loss_held[n - 1, 3])
        else:
            total = loss_acc[...]
        if n < len(LOSS_STEPS):
            where = LOSS_STEPS[n]
            mine, theirs = (0, 1) if len(where) == 1 else (place[where[0][0]],) * 2
            loss_held[n, mine] = total
            copies = []
            for j, name in enumerate(where):
                copy = remote(
                    loss_held.at[n, mine], loss_held.at[n, theirs], l_ss.at[n, j], l_rs.at[n, j], name
                )
                start(copy)
                copies.append(copy)
            loss_copies.append(copies)
        else:
            loss_out[0] = jnp.sum(total) / BATCH

    loss_step()

    parts = {"x": img_part, "y": txt_part}
    returns = {}
    for side in SIDES:
        for event in EVENTS:
            k, link = event
            n = INDEX[event] + (0 if side == "x" else len(EVENTS))
            entry = SENDS[link][k]
            at = n * 64
            returns[side, event] = remote(
                back_send.at[pl.ds(at, 64)], back_recv.at[pl.ds(at, 64)], b_ss.at[n], b_rs.at[n], side + BACK[link]
            )
    sibling = []

    def total_of(side, pair, off, first, last):
        at = POS[(pair, off)] * 128 + first
        value = parts[side][at : at + last - first, :]
        if side == "x":
            value = value + sib_recv[at : at + last - first, :].astype(F32)
        for event in EVENTS:
            k, link = event
            entry = SENDS[link][k]
            if entry == (pair, off, first, last):
                returns[side, event].wait_recv()
                n = INDEX[event] + (0 if side == "x" else len(EVENTS))
                value = value + back_recv[n * 64 : n * 64 + 64, :].astype(F32)
        return value

    def send_back(slot, sides):
        for event in RETURNS[slot]:
            for side in sides:
                k, link = event
                n = INDEX[event] + (0 if side == "x" else len(EVENTS))
                value = total_of(side, *landing(link, SENDS[link][k]))
                back_send[n * 64 : n * 64 + 64, :] = value.astype(BF16)
                start(returns[side, event])

    text_group(7, 8)
    send_back(0, "y")
    loss_step()
    sums[0].wait_recv()
    send_back(0, "x")
    image_group(5, 7)
    text_group(5, 7)
    send_back(1, "y")
    loss_step()
    sums[1].wait_recv()
    send_back(1, "x")
    image_group(4, 5)
    text_group(4, 5)
    send_back(2, "y")
    loss_step()
    sums[2].wait_recv()
    send_back(2, "x")
    image_group(1, 4)
    text_group(1, 4)
    send_back(3, "y")
    loss_step()
    sums[3].wait_recv()
    send_back(3, "x")
    send_back(4, "yx")
    image_group(0, 1)
    text_group(0, 1)
    sums[4].wait_recv()
    for half in (0, 64):
        for side, out in (("x", img_out), ("y", txt_out)):
            unit, inverse = normalize(raw[side][half : half + 64, :])
            direction = total_of(side, 0, 0, half, half + 64)
            along = jnp.sum(unit * direction, axis=-1, keepdims=True)
            out[half : half + 64, :] = inverse * (direction - unit * along)
    loss_step()
    for copy in pending:
        copy.wait_send()


def on_device(photo, sentence, photo_ids, sentence_ids, sharp, offset):
    vmem = pl.BlockSpec(memory_space=pltpu.VMEM)
    smem = pl.BlockSpec(memory_space=pltpu.SMEM)
    events = 2 * len(EVENTS)
    dma = pltpu.SemaphoreType.DMA
    return pl.pallas_call(
        kernel,
        out_shape=(
            pltpu.VMEM((ROWS, D), F32),
            pltpu.VMEM((ROWS, D), F32),
            jax.ShapeDtypeStruct((1,), F32),
        ),
        in_specs=[pl.BlockSpec(memory_space=pl.ANY)] * 2 + [vmem] * 2 + [smem] * 2,
        out_specs=(vmem, vmem, smem),
        scratch_shapes=[
            pltpu.VMEM((2048, D), BF16),
            pltpu.VMEM((1024, D), BF16),
            pltpu.VMEM((2048, 1024), BF16),
            pltpu.VMEM((1024, 2048), BF16),
            pltpu.VMEM((256, 896), F32),
            pltpu.VMEM((256, 896), F32),
            pltpu.VMEM((2048, 128), jnp.int32),
            pltpu.VMEM((1, 2048), jnp.int32),
            pltpu.VMEM((128, 128), jnp.int32),
            pltpu.VMEM((1, 1024), jnp.int32),
            pltpu.VMEM((1024, D), F32),
            pltpu.VMEM((1024, D), F32),
            pltpu.VMEM((8, 128), F32),
            pltpu.VMEM((1024, D), BF16),
            pltpu.VMEM((1024, D), BF16),
            pltpu.VMEM((events * 64, D), BF16),
            pltpu.VMEM((events * 64, D), BF16),
            pltpu.VMEM((2, 2, 4, 1, 128), jnp.int32),
            pltpu.VMEM((2, 4, 1, 128), jnp.int32),
            pltpu.VMEM((5, 4, 8, 128), F32),
            pltpu.VMEM((ROWS, D), BF16),
            pltpu.VMEM((ROWS, D), BF16),
            dma((2,)),
            dma((events,)), dma((events,)),
            dma((16,)), dma((16,)),
            dma((events,)), dma((events,)),
            dma((5,)), dma((5,)),
            dma((15,)), dma((15,)),
            dma((5, 3)), dma((5, 3)),
        ],
        compiler_params=pltpu.CompilerParams(
            collective_id=0, has_side_effects=True, vmem_limit_bytes=60 << 20
        ),
        cost_estimate=pl.CostEstimate(flops=3 * 2 * 2048 * 1024 * D, bytes_accessed=1 << 21, transcendentals=3 << 21),
        name="pair_loss",
    )(photo, sentence, photo_ids.reshape(1, ROWS), sentence_ids.reshape(1, ROWS), sharp, offset)


def solution(mesh):
    return jax.shard_map(
        on_device,
        mesh=mesh,
        in_specs=(
            P(("img", "txt"), None),
            P(("txt", "img"), None),
            P(("img", "txt")),
            P(("txt", "img")),
            P(),
            P(),
        ),
        out_specs=(P(("img", "txt"), None), P(("txt", "img"), None), P()),
        check_vma=False,
    )
```

```python
import functools

import jax
import jax.numpy as jnp
from jax import lax
from jax.experimental import pallas as pl
from jax.experimental.pallas import tpu as pltpu
from jax.sharding import PartitionSpec as P

MESH = pl.DeviceIdType.MESH
EPSILON = 1e-06
D = 1152
ROWS = 128
BATCH = 16384
F32 = jnp.float32
BF16 = jnp.bfloat16

POS = {(0, 0): 0, (0, 1): 1, (0, 3): 2, (1, 0): 3, (1, 1): 4, (0, 2): 5, (1, 3): 6, (1, 2): 7}
SENDS = {
    "R": [(0, 0, 64, 128), (0, 0, 0, 64), (1, 0, 0, 64), (0, 3, 64, 128), (1, 3, 0, 64)],
    "L": [(0, 0, 64, 128), (0, 0, 0, 64), (1, 0, 0, 64), (0, 1, 0, 64), (1, 1, 64, 128)],
    "V": [(0, 0, 0, 64), (0, 0, 64, 128), (0, 1, 64, 128), (0, 3, 64, 128)],
}
EVENTS = [(k, link) for k in range(5) for link in "RLV" if k < len(SENDS[link])]
INDEX = {event: i for i, event in enumerate(EVENTS)}
BACK = {"R": "L", "L": "R", "V": "V"}
RETURNS = [
    [(4, "R"), (4, "L")],
    [(3, "R"), (3, "L"), (3, "V")],
    [(2, "R"), (2, "L"), (2, "V")],
    [(1, "R"), (1, "L"), (1, "V")],
    [(0, "R"), (0, "L"), (0, "V")],
]
SIDES = "xy"


def landing(link, entry):
    pair, offset, first, last = entry
    if link == "R":
        return (pair, (offset + 3) % 4, first, last)
    if link == "L":
        return (pair, (offset + 1) % 4, first, last)
    return (1 - pair, offset, first, last)


ENTRIES = {SENDS[link][k] for k, link in EVENTS}
LEAVES = {
    POS[place[:2]] * 128 + place[2]: (k, link)
    for k, link in EVENTS
    for place in [landing(link, SENDS[link][k])]
    if place not in ENTRIES
}
SLICE = 16
TURNED = {4: 0, 7: 128}


def partners():
    i = lax.axis_index("img")
    t = lax.axis_index("txt")
    z, c, y, x = i // 2, i % 2, t // 4, t % 4

    def at(x, y, z, c):
        return (z * 2 + c, y * 4 + x)

    return {
        "xR": at((x + 1) % 4, y, z, c),
        "xL": at((x + 3) % 4, y, z, c),
        "xV": at(x, y, z + 1 - 2 * (z % 2), c),
        "x2": at((x + 2) % 4, y, z, c),
        "xVR": at((x + 1) % 4, y, z + 1 - 2 * (z % 2), c),
        "xVL": at((x + 3) % 4, y, z + 1 - 2 * (z % 2), c),
        "xV2": at((x + 2) % 4, y, z + 1 - 2 * (z % 2), c),
        "yR": at(x, (y + 1) % 4, z, c),
        "yL": at(x, (y + 3) % 4, z, c),
        "yV": at(x, y, 3 - z, c),
        "y2": at(x, (y + 2) % 4, z, c),
        "yVR": at(x, (y + 1) % 4, 3 - z, c),
        "yVL": at(x, (y + 3) % 4, 3 - z, c),
        "yV2": at(x, (y + 2) % 4, 3 - z, c),
        "sib": at(x, y, z, 1 - c),
    }


PLACES = {"R": (0, 3), "L": (0, 1), "2": (0, 2), "V": (1, 0), "VR": (1, 3), "VL": (1, 1), "V2": (1, 2)}
BARRIER = tuple(side + name for side in SIDES for name in PLACES) + ("sib",)
LOSS_STEPS = (("sib",), ("xV",), ("yV",), ("xR", "xL", "x2"), ("yR", "yL", "y2"))


def normalize(values):
    wide = values.astype(F32)
    inverse = lax.rsqrt(jnp.sum(wide * wide, axis=-1, keepdims=True) + EPSILON)
    return wide * inverse, inverse


def kernel(
    img_hbm, txt_hbm, img_ids, txt_ids, sharp_ref, offset_ref,
    img_out, txt_out, loss_out,
    images, texts, coef, coef_t, score0, score1, img_rows, img_lanes, txt_rows, txt_lanes, img_part, txt_part, loss_acc,
    sib_send, sib_recv, back_send, back_recv, idx, idt, loss_held,
    img_raw, txt_raw, in_sem, g_ss, g_rs, f_ss, f_rs, b_ss, b_rs, p_ss, p_rs, i_ss, i_rs, l_ss, l_rs,
):
    to = partners()
    sharp = sharp_ref[0]
    offset = offset_ref[0]
    raw = {"x": img_raw, "y": txt_raw}

    def remote(src, dst, send, recv, where):
        return pltpu.make_async_remote_copy(
            src_ref=src, dst_ref=dst, send_sem=send, recv_sem=recv, device_id=to[where], device_id_type=MESH
        )

    pending = []

    def start(copy):
        copy.start()
        pending.append(copy)

    barrier = pltpu.get_barrier_semaphore()
    for name in BARRIER:
        pl.semaphore_signal(barrier, inc=1, device_id=to[name], device_id_type=MESH)
    img_load = pltpu.make_async_copy(img_hbm, img_raw, in_sem.at[0])
    txt_load = pltpu.make_async_copy(txt_hbm, txt_raw, in_sem.at[1])
    img_load.start()
    txt_load.start()
    img_load.wait()
    images[0:ROWS, :] = normalize(img_raw[...])[0].astype(BF16)
    txt_load.wait()
    texts[0:ROWS, :] = normalize(txt_raw[...])[0].astype(BF16)
    idx[0, 0, 0] = img_ids[...]
    idt[0, 0] = txt_ids[...]
    pl.semaphore_wait(barrier, len(BARRIER))

    def rows_of(side, entry):
        pair, off, first, last = entry
        pos = POS[(pair, off)]
        if side == "x":
            return images.at[pl.ds(pos * 128 + first, last - first)]
        return texts.at[pl.ds(pos * 128 + first, last - first)]

    gather = {}
    for side in SIDES:
        for event in EVENTS:
            k, link = event
            n = INDEX[event] + (0 if side == "x" else len(EVENTS))
            entry = SENDS[link][k]
            gather[side, event] = remote(
                rows_of(side, entry), rows_of(side, landing(link, entry)), g_ss.at[n], g_rs.at[n], side + link
            )

    forwards = {}

    def forward(entry):
        n = sum(len(copies) for copies in forwards.values())
        pair, off, first, last = entry
        at = POS[(pair, off)] * 128 + first
        copy = remote(
            images.at[pl.ds(at, last - first)], images.at[pl.ds(at + 1024, last - first)], f_ss.at[n], f_rs.at[n], "sib"
        )
        start(copy)
        forwards.setdefault(POS[(pair, off)], []).append(copy)

    def send_slot(k):
        for event in EVENTS:
            if event[0] == k:
                for side in SIDES:
                    start(gather[side, event])

    def receive_slot(k):
        for event in EVENTS:
            if event[0] == k:
                for side in SIDES:
                    gather[side, event].wait_recv()
                forward(landing(event[1], SENDS[event[1]][k]))

    def receive_sibling(*positions):
        for pos in positions:
            for copy in forwards[pos]:
                copy.wait_recv()

    id_copies = []
    for name, place in PLACES.items():
        for side, ids in (("x", idx.at[0]), ("y", idt)):
            n = len(id_copies)
            id_copies.append(remote(ids.at[0, 0], ids.at[place], i_ss.at[n], i_rs.at[n], side + name))
            start(id_copies[n])
    send_slot(0)
    send_slot(1)
    forward((0, 0, 0, 128))
    for copy in id_copies:
        copy.wait_recv()
    id_forward = remote(idx.at[0], idx.at[1], i_ss.at[14], i_rs.at[14], "sib")
    start(id_forward)
    for (pair, off), pos in POS.items():
        txt_lanes[:, pos * 128 : pos * 128 + 128] = idt[pair, off]
        if pos in TURNED:
            at = TURNED[pos]
            txt_rows[at : at + 128, :] = jnp.broadcast_to(idt[pair, off], (128, 128)).T

    def spread(kind):
        for (pair, off), pos in POS.items():
            at = kind * 1024 + pos * 128
            img_lanes[:, at : at + 128] = idx[kind, pair, off]
            img_rows[at : at + 128, :] = jnp.broadcast_to(idx[kind, pair, off], (128, 128)).T

    receive_slot(0)
    send_slot(2)
    spread(0)
    id_forward.wait_recv()
    spread(1)
    receive_slot(1)
    send_slot(3)

    sums = []

    def image_group(first, last):
        n = len(sums)
        size = (last - first) * 128
        own = slice(first * 128, last * 128)
        other = slice(1024 + first * 128, 1024 + last * 128)
        both = jnp.concatenate([coef[own, :], coef[other, :]], axis=0)
        full = jnp.dot(both, texts[...], preferred_element_type=F32)
        img_part[own, :] = full[:size]
        sib_send[own, :] = full[size:].astype(BF16)
        rows = pl.ds(first * 128, (last - first) * 128)
        sums.append(remote(sib_send.at[rows], sib_recv.at[rows], p_ss.at[n], p_rs.at[n], "sib"))

    def text_group(first, last):
        rows = slice(first * 128, last * 128)
        full = jnp.dot(coef_t[rows, :], images[...], preferred_element_type=F32)
        for half in range(first * 128, last * 128, 64):
            value = full[half - first * 128 : half - first * 128 + 64]
            if half in LEAVES:
                n = INDEX[LEAVES[half]] + len(EVENTS)
                back_send[n * 64 : n * 64 + 64, :] = value.astype(BF16)
            else:
                txt_part[half : half + 64, :] = value

    loss_acc[...] = jnp.zeros_like(loss_acc)

    def product(tile, out):
        texts_first, row, height, col, width = tile
        left, right = (texts, images) if texts_first else (images, texts)
        out[0:height, 0:width] = lax.dot_general(
            left[row : row + height, :],
            right[col : col + width, :],
            (((1,), (1,)), ((), ())),
            preferred_element_type=F32,
        )

    def pointwise(tile, scored):
        texts_first, row, height, col, width = tile
        if texts_first:
            out, out_t, lanes, row_ids = coef_t, coef, img_lanes, txt_rows
            row_ids_at = TURNED[row // 128]
        else:
            out, out_t, lanes, row_ids = coef, coef_t, txt_lanes, img_rows
            row_ids_at = row
        summed = loss_acc[...]
        for left in range(0, width, 512):
            wide = min(512, width - left)
            cols = slice(col + left, col + left + wide)
            ids = lanes[:, cols]
            for q in range(height // SLICE):
                block = row_ids[row_ids_at + q * SLICE : row_ids_at + (q + 1) * SLICE, :]
                positive = jnp.concatenate([block] * (wide // 128), axis=1) == ids
                scale = jnp.where(positive, -sharp, sharp)
                shift = jnp.where(positive, -offset, offset)
                grown = jnp.exp(scale * scored[q * SLICE : (q + 1) * SLICE, left : left + wide] + shift)
                above = 1.0 + grown
                share = grown * pl.reciprocal(above, approx=True)
                out[row + q * SLICE : row + (q + 1) * SLICE, cols] = (share * scale).astype(BF16)
                if q % 8 == 0:
                    small = grown
                    logs = jnp.log(above)
                else:
                    small = small + grown
                    logs = logs + jnp.log(above)
                if q == 7:
                    total = jnp.where(small < 1e-3, small, logs)
                elif q % 8 == 7:
                    total = total + jnp.where(small < 1e-3, small, logs)
            for a in range(0, SLICE, 8):
                for b in range(0, wide, 128):
                    summed = summed + total[a : a + 8, b : b + 128]
        loss_acc[...] = summed
        rows = slice(row, row + height)
        cols = slice(col, col + width)
        out_t[cols, rows] = out[rows, cols].T

    scores = (score0, score1)
    done = []

    def score(*tiles):
        for tile in tiles:
            product(tile, scores[len(done) % 2])
            if done:
                pointwise(done[-1], scores[(len(done) - 1) % 2])
            done.append(tile)

    score((False, 0, 512, 0, 512))
    receive_sibling(0, 1, 2, 3)
    score((False, 1024, 512, 0, 512))
    receive_slot(2)
    send_slot(4)
    score((False, 512, 128, 0, 512), (True, 512, 128, 0, 640))
    receive_sibling(4)
    score((False, 1536, 128, 0, 512), (True, 512, 128, 1024, 640))
    receive_slot(3)
    score((False, 0, 640, 640, 256), (False, 1024, 640, 640, 256))
    score((False, 640, 256, 0, 512), (False, 640, 256, 512, 384))
    receive_sibling(5, 6)
    receive_slot(4)
    score((False, 1664, 256, 0, 512), (False, 1664, 256, 512, 384))
    score((False, 896, 128, 0, 1024), (True, 896, 128, 0, 896))
    receive_sibling(7)
    score((False, 1920, 128, 0, 1024), (True, 896, 128, 1024, 896))
    image_group(7, 8)
    start(sums[0])
    pointwise(done[-1], scores[(len(done) - 1) % 2])

    place = {"x": lax.axis_index("txt") % 4, "y": lax.axis_index("txt") // 4}
    loss_copies = []

    def loss_step():
        n = len(loss_copies)
        if n:
            for copy in loss_copies[-1]:
                copy.wait_recv()
            before = LOSS_STEPS[n - 1]
            if len(before) == 1:
                total = loss_held[n - 1, 0] + loss_held[n - 1, 1]
            else:
                total = (loss_held[n - 1, 0] + loss_held[n - 1, 1]) + (loss_held[n - 1, 2] + loss_held[n - 1, 3])
        else:
            total = loss_acc[...]
        if n < len(LOSS_STEPS):
            where = LOSS_STEPS[n]
            mine, theirs = (0, 1) if len(where) == 1 else (place[where[0][0]],) * 2
            loss_held[n, mine] = total
            copies = []
            for j, name in enumerate(where):
                copy = remote(
                    loss_held.at[n, mine], loss_held.at[n, theirs], l_ss.at[n, j], l_rs.at[n, j], name
                )
                start(copy)
                copies.append(copy)
            loss_copies.append(copies)
        else:
            loss_out[0] = jnp.sum(total) / BATCH

    loss_step()

    parts = {"x": img_part, "y": txt_part}
    returns = {}
    for side in SIDES:
        for event in EVENTS:
            k, link = event
            n = INDEX[event] + (0 if side == "x" else len(EVENTS))
            entry = SENDS[link][k]
            at = n * 64
            returns[side, event] = remote(
                back_send.at[pl.ds(at, 64)], back_recv.at[pl.ds(at, 64)], b_ss.at[n], b_rs.at[n], side + BACK[link]
            )
    sibling = []

    def total_of(side, pair, off, first, last):
        at = POS[(pair, off)] * 128 + first
        value = parts[side][at : at + last - first, :]
        if side == "x":
            value = value + sib_recv[at : at + last - first, :].astype(F32)
        for event in EVENTS:
            k, link = event
            entry = SENDS[link][k]
            if entry == (pair, off, first, last):
                returns[side, event].wait_recv()
                n = INDEX[event] + (0 if side == "x" else len(EVENTS))
                value = value + back_recv[n * 64 : n * 64 + 64, :].astype(F32)
        return value

    def send_back(slot, sides):
        for event in RETURNS[slot]:
            for side in sides:
                k, link = event
                n = INDEX[event] + (0 if side == "x" else len(EVENTS))
                if side == "x" or event not in LEAVES.values():
                    value = total_of(side, *landing(link, SENDS[link][k]))
                    back_send[n * 64 : n * 64 + 64, :] = value.astype(BF16)
                start(returns[side, event])

    text_group(7, 8)
    image_group(5, 7)
    start(sums[1])
    loss_step()
    send_back(0, "y")
    sums[0].wait_recv()
    send_back(0, "x")
    text_group(5, 7)
    image_group(4, 5)
    start(sums[2])
    loss_step()
    send_back(1, "y")
    sums[1].wait_recv()
    send_back(1, "x")
    text_group(4, 5)
    image_group(1, 4)
    start(sums[3])
    loss_step()
    send_back(2, "y")
    sums[2].wait_recv()
    send_back(2, "x")
    text_group(1, 4)
    loss_step()
    send_back(3, "y")
    sums[3].wait_recv()
    send_back(3, "x")
    send_back(4, "yx")
    image_group(0, 1)
    start(sums[4])
    text_group(0, 1)
    sums[4].wait_recv()
    for half in (0, 64):
        for side, out in (("x", img_out), ("y", txt_out)):
            unit, inverse = normalize(raw[side][half : half + 64, :])
            direction = total_of(side, 0, 0, half, half + 64)
            along = jnp.sum(unit * direction, axis=-1, keepdims=True)
            out[half : half + 64, :] = inverse * (direction - unit * along)
    loss_step()
    for copy in pending:
        copy.wait_send()


def on_device(photo, sentence, photo_ids, sentence_ids, sharp, offset):
    vmem = pl.BlockSpec(memory_space=pltpu.VMEM)
    smem = pl.BlockSpec(memory_space=pltpu.SMEM)
    events = 2 * len(EVENTS)
    dma = pltpu.SemaphoreType.DMA
    return pl.pallas_call(
        kernel,
        out_shape=(
            pltpu.VMEM((ROWS, D), F32),
            pltpu.VMEM((ROWS, D), F32),
            jax.ShapeDtypeStruct((1,), F32),
        ),
        in_specs=[pl.BlockSpec(memory_space=pl.ANY)] * 2 + [vmem] * 2 + [smem] * 2,
        out_specs=(vmem, vmem, smem),
        scratch_shapes=[
            pltpu.VMEM((2048, D), BF16),
            pltpu.VMEM((1024, D), BF16),
            pltpu.VMEM((2048, 1024), BF16),
            pltpu.VMEM((1024, 2048), BF16),
            pltpu.VMEM((640, 1024), F32),
            pltpu.VMEM((640, 1024), F32),
            pltpu.VMEM((2048, 128), jnp.int32),
            pltpu.VMEM((1, 2048), jnp.int32),
            pltpu.VMEM((256, 128), jnp.int32),
            pltpu.VMEM((1, 1024), jnp.int32),
            pltpu.VMEM((1024, D), F32),
            pltpu.VMEM((1024, D), F32),
            pltpu.VMEM((8, 128), F32),
            pltpu.VMEM((1024, D), BF16),
            pltpu.VMEM((1024, D), BF16),
            pltpu.VMEM((events * 64, D), BF16),
            pltpu.VMEM((events * 64, D), BF16),
            pltpu.VMEM((2, 2, 4, 1, 128), jnp.int32),
            pltpu.VMEM((2, 4, 1, 128), jnp.int32),
            pltpu.VMEM((5, 4, 8, 128), F32),
            pltpu.VMEM((ROWS, D), BF16),
            pltpu.VMEM((ROWS, D), BF16),
            dma((2,)),
            dma((events,)), dma((events,)),
            dma((16,)), dma((16,)),
            dma((events,)), dma((events,)),
            dma((5,)), dma((5,)),
            dma((15,)), dma((15,)),
            dma((5, 3)), dma((5, 3)),
        ],
        compiler_params=pltpu.CompilerParams(
            collective_id=0, has_side_effects=True, vmem_limit_bytes=60 << 20
        ),
        cost_estimate=pl.CostEstimate(flops=3 * 2 * 2048 * 1024 * D, bytes_accessed=1 << 21, transcendentals=3 << 21),
        name="pair_loss",
    )(photo, sentence, photo_ids.reshape(1, ROWS), sentence_ids.reshape(1, ROWS), sharp, offset)


def solution(mesh):
    return jax.shard_map(
        on_device,
        mesh=mesh,
        in_specs=(
            P(("img", "txt"), None),
            P(("txt", "img"), None),
            P(("img", "txt")),
            P(("txt", "img")),
            P(),
            P(),
        ),
        out_specs=(P(("img", "txt"), None), P(("txt", "img"), None), P()),
        check_vma=False,
    )
```

```python
import functools

import jax
import jax.numpy as jnp
from jax import lax
from jax.experimental import pallas as pl
from jax.experimental.pallas import tpu as pltpu
from jax.sharding import PartitionSpec as P

MESH = pl.DeviceIdType.MESH
EPSILON = 1e-06
D = 1152
ROWS = 128
BATCH = 16384
F32 = jnp.float32
BF16 = jnp.bfloat16

POS = {(0, 0): 0, (0, 1): 1, (0, 3): 2, (1, 0): 3, (1, 1): 4, (0, 2): 5, (1, 3): 6, (1, 2): 7}
SENDS = {
    "R": [(0, 0, 64, 128), (0, 0, 0, 64), (1, 0, 0, 64), (0, 3, 64, 128), (1, 3, 0, 64)],
    "L": [(0, 0, 64, 128), (0, 0, 0, 64), (1, 0, 0, 64), (0, 1, 0, 64), (1, 1, 64, 128)],
    "V": [(0, 0, 0, 64), (0, 0, 64, 128), (0, 1, 64, 128), (0, 3, 64, 128)],
}
EVENTS = [(k, link) for k in range(5) for link in "RLV" if k < len(SENDS[link])]
INDEX = {event: i for i, event in enumerate(EVENTS)}
BACK = {"R": "L", "L": "R", "V": "V"}
RETURNS = [
    [(4, "R"), (4, "L")],
    [(3, "R"), (3, "L"), (3, "V")],
    [(2, "R"), (2, "L"), (2, "V")],
    [(1, "R"), (1, "L"), (1, "V")],
    [(0, "R"), (0, "L"), (0, "V")],
]
SIDES = "xy"


def landing(link, entry):
    pair, offset, first, last = entry
    if link == "R":
        return (pair, (offset + 3) % 4, first, last)
    if link == "L":
        return (pair, (offset + 1) % 4, first, last)
    return (1 - pair, offset, first, last)


ENTRIES = {SENDS[link][k] for k, link in EVENTS}
LEAVES = {
    POS[place[:2]] * 128 + place[2]: (k, link)
    for k, link in EVENTS
    for place in [landing(link, SENDS[link][k])]
    if place not in ENTRIES
}
SLICE = 16
TURNED = {4: 0, 7: 128}


def partners():
    i = lax.axis_index("img")
    t = lax.axis_index("txt")
    z, c, y, x = i // 2, i % 2, t // 4, t % 4

    def at(x, y, z, c):
        return (z * 2 + c, y * 4 + x)

    return {
        "xR": at((x + 1) % 4, y, z, c),
        "xL": at((x + 3) % 4, y, z, c),
        "xV": at(x, y, z + 1 - 2 * (z % 2), c),
        "x2": at((x + 2) % 4, y, z, c),
        "xVR": at((x + 1) % 4, y, z + 1 - 2 * (z % 2), c),
        "xVL": at((x + 3) % 4, y, z + 1 - 2 * (z % 2), c),
        "xV2": at((x + 2) % 4, y, z + 1 - 2 * (z % 2), c),
        "yR": at(x, (y + 1) % 4, z, c),
        "yL": at(x, (y + 3) % 4, z, c),
        "yV": at(x, y, 3 - z, c),
        "y2": at(x, (y + 2) % 4, z, c),
        "yVR": at(x, (y + 1) % 4, 3 - z, c),
        "yVL": at(x, (y + 3) % 4, 3 - z, c),
        "yV2": at(x, (y + 2) % 4, 3 - z, c),
        "sib": at(x, y, z, 1 - c),
        "z2": at(x, y, (z + 2) % 4, c),
        "z1s": at(x, y, z + 1 - 2 * (z % 2), 1 - c),
        "z2s": at(x, y, (z + 2) % 4, 1 - c),
        "z3s": at(x, y, 3 - z, 1 - c),
    }


PLACES = {"R": (0, 3), "L": (0, 1), "2": (0, 2), "V": (1, 0), "VR": (1, 3), "VL": (1, 1), "V2": (1, 2)}
BARRIER = tuple(side + name for side in SIDES for name in PLACES) + ("sib", "z2", "z1s", "z2s", "z3s")
LOSS_STEPS = (("xR", "xL", "x2"), ("yR", "yL", "y2"), ("xV", "yV", "z2", "sib", "z1s", "z2s", "z3s"))


def normalize(values):
    wide = values.astype(F32)
    inverse = lax.rsqrt(jnp.sum(wide * wide, axis=-1, keepdims=True) + EPSILON)
    return wide * inverse, inverse


def kernel(
    img_hbm, txt_hbm, img_ids, txt_ids, sharp_ref, offset_ref,
    img_out, txt_out, loss_out,
    images, texts, coef, coef_t, score0, score1, img_rows, img_lanes, txt_rows, txt_lanes, img_part, txt_part, loss_acc,
    sib_send, sib_recv, back_send, back_recv, idx, idt, loss_held,
    img_unit, img_inverse, txt_unit, txt_inverse, img_raw, txt_raw, in_sem, g_ss, g_rs, f_ss, f_rs, b_ss, b_rs, p_ss, p_rs, i_ss, i_rs, l_ss, l_rs,
):
    to = partners()
    sharp = sharp_ref[0]
    offset = offset_ref[0]
    raw = {"x": img_raw, "y": txt_raw}

    def remote(src, dst, send, recv, where):
        return pltpu.make_async_remote_copy(
            src_ref=src, dst_ref=dst, send_sem=send, recv_sem=recv, device_id=to[where], device_id_type=MESH
        )

    pending = []

    def start(copy):
        copy.start()
        pending.append(copy)

    barrier = pltpu.get_barrier_semaphore()
    for name in BARRIER:
        pl.semaphore_signal(barrier, inc=1, device_id=to[name], device_id_type=MESH)
    img_load = pltpu.make_async_copy(img_hbm, img_raw, in_sem.at[0])
    txt_load = pltpu.make_async_copy(txt_hbm, txt_raw, in_sem.at[1])
    img_load.start()
    txt_load.start()
    img_load.wait()
    images[0:ROWS, :] = normalize(img_raw[...])[0].astype(BF16)
    txt_load.wait()
    texts[0:ROWS, :] = normalize(txt_raw[...])[0].astype(BF16)
    idx[0, 0, 0] = img_ids[...]
    idt[0, 0] = txt_ids[...]
    pl.semaphore_wait(barrier, len(BARRIER))

    def rows_of(side, entry):
        pair, off, first, last = entry
        pos = POS[(pair, off)]
        if side == "x":
            return images.at[pl.ds(pos * 128 + first, last - first)]
        return texts.at[pl.ds(pos * 128 + first, last - first)]

    gather = {}
    for side in SIDES:
        for event in EVENTS:
            k, link = event
            n = INDEX[event] + (0 if side == "x" else len(EVENTS))
            entry = SENDS[link][k]
            gather[side, event] = remote(
                rows_of(side, entry), rows_of(side, landing(link, entry)), g_ss.at[n], g_rs.at[n], side + link
            )

    forwards = {}

    def forward(entry):
        n = sum(len(copies) for copies in forwards.values())
        pair, off, first, last = entry
        at = POS[(pair, off)] * 128 + first
        copy = remote(
            images.at[pl.ds(at, last - first)], images.at[pl.ds(at + 1024, last - first)], f_ss.at[n], f_rs.at[n], "sib"
        )
        start(copy)
        forwards.setdefault(POS[(pair, off)], []).append(copy)

    def send_slot(k):
        for event in EVENTS:
            if event[0] == k:
                for side in SIDES:
                    start(gather[side, event])

    def receive_slot(k):
        for event in EVENTS:
            if event[0] == k:
                for side in SIDES:
                    gather[side, event].wait_recv()
                forward(landing(event[1], SENDS[event[1]][k]))

    def receive_sibling(*positions):
        for pos in positions:
            for copy in forwards[pos]:
                copy.wait_recv()

    id_copies = []
    for name, place in PLACES.items():
        for side, ids in (("x", idx.at[0]), ("y", idt)):
            n = len(id_copies)
            id_copies.append(remote(ids.at[0, 0], ids.at[place], i_ss.at[n], i_rs.at[n], side + name))
            start(id_copies[n])
    send_slot(0)
    send_slot(1)
    forward((0, 0, 0, 128))
    for side, unit_ref, inverse_ref in (("x", img_unit, img_inverse), ("y", txt_unit, txt_inverse)):
        unit_ref[...], inverse_ref[...] = normalize(raw[side][...])
    for copy in id_copies:
        copy.wait_recv()
    id_forward = remote(idx.at[0], idx.at[1], i_ss.at[14], i_rs.at[14], "sib")
    start(id_forward)
    for (pair, off), pos in POS.items():
        txt_lanes[:, pos * 128 : pos * 128 + 128] = idt[pair, off]
        if pos in TURNED:
            at = TURNED[pos]
            txt_rows[at : at + 128, :] = jnp.broadcast_to(idt[pair, off], (128, 128)).T

    def spread(kind):
        for (pair, off), pos in POS.items():
            at = kind * 1024 + pos * 128
            img_lanes[:, at : at + 128] = idx[kind, pair, off]
            img_rows[at : at + 128, :] = jnp.broadcast_to(idx[kind, pair, off], (128, 128)).T

    receive_slot(0)
    send_slot(2)
    spread(0)
    id_forward.wait_recv()
    spread(1)
    receive_slot(1)
    send_slot(3)

    sums = []

    def image_group(first, last):
        n = len(sums)
        size = (last - first) * 128
        own = slice(first * 128, last * 128)
        other = slice(1024 + first * 128, 1024 + last * 128)
        both = jnp.concatenate([coef[own, :], coef[other, :]], axis=0)
        full = jnp.dot(both, texts[...], preferred_element_type=F32)
        img_part[own, :] = full[:size]
        sib_send[own, :] = full[size:].astype(BF16)
        rows = pl.ds(first * 128, (last - first) * 128)
        sums.append(remote(sib_send.at[rows], sib_recv.at[rows], p_ss.at[n], p_rs.at[n], "sib"))

    def text_group(first, last):
        rows = slice(first * 128, last * 128)
        full = jnp.dot(coef_t[rows, :], images[...], preferred_element_type=F32)
        for half in range(first * 128, last * 128, 64):
            value = full[half - first * 128 : half - first * 128 + 64]
            if half in LEAVES:
                n = INDEX[LEAVES[half]] + len(EVENTS)
                back_send[n * 64 : n * 64 + 64, :] = value.astype(BF16)
            else:
                txt_part[half : half + 64, :] = value

    loss_acc[...] = jnp.zeros_like(loss_acc)

    def product(tile, out):
        texts_first, row, height, col, width = tile
        left, right = (texts, images) if texts_first else (images, texts)
        out[0:height, 0:width] = lax.dot_general(
            left[row : row + height, :],
            right[col : col + width, :],
            (((1,), (1,)), ((), ())),
            preferred_element_type=F32,
        )

    def pointwise(tile, scored):
        texts_first, row, height, col, width = tile
        if texts_first:
            out, out_t, lanes, row_ids = coef_t, coef, img_lanes, txt_rows
            row_ids_at = TURNED[row // 128]
        else:
            out, out_t, lanes, row_ids = coef, coef_t, txt_lanes, img_rows
            row_ids_at = row
        summed = loss_acc[...]
        for left in range(0, width, 512):
            wide = min(512, width - left)
            cols = slice(col + left, col + left + wide)
            ids = lanes[:, cols]
            for q in range(height // SLICE):
                block = row_ids[row_ids_at + q * SLICE : row_ids_at + (q + 1) * SLICE, :]
                positive = jnp.concatenate([block] * (wide // 128), axis=1) == ids
                scale = jnp.where(positive, -sharp, sharp)
                shift = jnp.where(positive, -offset, offset)
                grown = jnp.exp(scale * scored[q * SLICE : (q + 1) * SLICE, left : left + wide] + shift)
                above = 1.0 + grown
                share = grown * pl.reciprocal(above, approx=True)
                out[row + q * SLICE : row + (q + 1) * SLICE, cols] = (share * scale).astype(BF16)
                if q % 8 == 0:
                    small = grown
                    logs = jnp.log(above)
                else:
                    small = small + grown
                    logs = logs + jnp.log(above)
                if q == 7:
                    total = jnp.where(small < 1e-3, small, logs)
                elif q % 8 == 7:
                    total = total + jnp.where(small < 1e-3, small, logs)
            for a in range(0, SLICE, 8):
                for b in range(0, wide, 128):
                    summed = summed + total[a : a + 8, b : b + 128]
        loss_acc[...] = summed
        rows = slice(row, row + height)
        cols = slice(col, col + width)
        out_t[cols, rows] = out[rows, cols].T

    scores = (score0, score1)
    done = []

    def score(*tiles):
        for tile in tiles:
            product(tile, scores[len(done) % 2])
            if done:
                pointwise(done[-1], scores[(len(done) - 1) % 2])
            done.append(tile)

    score((False, 0, 512, 0, 512))
    receive_sibling(0, 1, 2, 3)
    score((False, 1024, 512, 0, 512))
    receive_slot(2)
    send_slot(4)
    score((False, 512, 128, 0, 512), (True, 512, 128, 0, 640))
    receive_sibling(4)
    score((False, 1536, 128, 0, 512), (True, 512, 128, 1024, 640))
    receive_slot(3)
    score((False, 0, 640, 640, 256), (False, 1024, 640, 640, 256))
    score((False, 640, 256, 0, 512), (False, 640, 256, 512, 384))
    receive_sibling(5, 6)
    receive_slot(4)
    score((False, 1664, 256, 0, 512), (False, 1664, 256, 512, 384))
    score((False, 896, 128, 0, 1024), (True, 896, 128, 0, 896))
    receive_sibling(7)
    score((False, 1920, 128, 0, 1024), (True, 896, 128, 1024, 896))
    image_group(7, 8)
    pointwise(done[-1], scores[(len(done) - 1) % 2])
    start(sums[0])

    places = (lax.axis_index("txt") % 4, lax.axis_index("txt") // 4, lax.axis_index("img"))
    loss_copies = []

    def loss_step():
        n = len(loss_copies)
        if n:
            for copy in loss_copies[-1]:
                copy.wait_recv()
            total = loss_held[n - 1, 0]
            for j in range(len(LOSS_STEPS[n - 1])):
                total = total + loss_held[n - 1, j + 1]
        else:
            total = loss_acc[...]
        if n < len(LOSS_STEPS):
            loss_held[n, places[n]] = total
            copies = []
            for j, name in enumerate(LOSS_STEPS[n]):
                mine = loss_held.at[n, places[n]]
                copy = remote(mine, mine, l_ss.at[n, j], l_rs.at[n, j], name)
                start(copy)
                copies.append(copy)
            loss_copies.append(copies)
        else:
            loss_out[0] = jnp.sum(total) / BATCH

    parts = {"x": img_part, "y": txt_part}
    returns = {}
    for side in SIDES:
        for event in EVENTS:
            k, link = event
            n = INDEX[event] + (0 if side == "x" else len(EVENTS))
            entry = SENDS[link][k]
            at = n * 64
            returns[side, event] = remote(
                back_send.at[pl.ds(at, 64)], back_recv.at[pl.ds(at, 64)], b_ss.at[n], b_rs.at[n], side + BACK[link]
            )
    sibling = []

    def total_of(side, pair, off, first, last):
        added = [event for event in EVENTS if SENDS[event[1]][event[0]] == (pair, off, first, last)]
        for event in added:
            returns[side, event].wait_recv()
        at = POS[(pair, off)] * 128 + first
        value = parts[side][at : at + last - first, :]
        if side == "x":
            value = value + sib_recv[at : at + last - first, :].astype(F32)
        for event in added:
            n = INDEX[event] + (0 if side == "x" else len(EVENTS))
            value = value + back_recv[n * 64 : n * 64 + 64, :].astype(F32)
        return value

    def send_back(slot, sides):
        for event in RETURNS[slot]:
            for side in sides:
                k, link = event
                n = INDEX[event] + (0 if side == "x" else len(EVENTS))
                if side == "x" or event not in LEAVES.values():
                    value = total_of(side, *landing(link, SENDS[link][k]))
                    back_send[n * 64 : n * 64 + 64, :] = value.astype(BF16)
                start(returns[side, event])

    text_group(7, 8)
    image_group(5, 7)
    start(sums[1])
    loss_step()
    send_back(0, "y")
    sums[0].wait_recv()
    send_back(0, "x")
    text_group(5, 7)
    image_group(4, 5)
    start(sums[2])
    send_back(1, "y")
    sums[1].wait_recv()
    send_back(1, "x")
    text_group(4, 5)
    image_group(1, 4)
    start(sums[3])
    loss_step()
    send_back(2, "y")
    sums[2].wait_recv()
    send_back(2, "x")
    text_group(1, 4)
    loss_step()
    send_back(3, "y")
    sums[3].wait_recv()
    send_back(3, "x")
    send_back(4, "yx")
    image_group(0, 1)
    start(sums[4])
    text_group(0, 1)
    sums[4].wait_recv()
    for copy in pending:
        copy.wait_send()
    loss_step()
    ends = (("x", img_out, img_unit, img_inverse), ("y", txt_out, txt_unit, txt_inverse))
    for half in (0, 64):
        for side, out, unit_ref, inverse_ref in ends:
            direction = total_of(side, 0, 0, half, half + 64)
            unit = unit_ref[half : half + 64, :]
            along = jnp.sum(unit * direction, axis=-1, keepdims=True)
            out[half : half + 64, :] = inverse_ref[half : half + 64, :] * (direction - unit * along)


def on_device(photo, sentence, photo_ids, sentence_ids, sharp, offset):
    vmem = pl.BlockSpec(memory_space=pltpu.VMEM)
    smem = pl.BlockSpec(memory_space=pltpu.SMEM)
    events = 2 * len(EVENTS)
    dma = pltpu.SemaphoreType.DMA
    return pl.pallas_call(
        kernel,
        out_shape=(
            pltpu.VMEM((ROWS, D), F32),
            pltpu.VMEM((ROWS, D), F32),
            jax.ShapeDtypeStruct((1,), F32),
        ),
        in_specs=[pl.BlockSpec(memory_space=pl.ANY)] * 2 + [vmem] * 2 + [smem] * 2,
        out_specs=(vmem, vmem, smem),
        scratch_shapes=[
            pltpu.VMEM((2048, D), BF16),
            pltpu.VMEM((1024, D), BF16),
            pltpu.VMEM((2048, 1024), BF16),
            pltpu.VMEM((1024, 2048), BF16),
            pltpu.VMEM((640, 1024), F32),
            pltpu.VMEM((640, 1024), F32),
            pltpu.VMEM((2048, 128), jnp.int32),
            pltpu.VMEM((1, 2048), jnp.int32),
            pltpu.VMEM((256, 128), jnp.int32),
            pltpu.VMEM((1, 1024), jnp.int32),
            pltpu.VMEM((1024, D), F32),
            pltpu.VMEM((1024, D), F32),
            pltpu.VMEM((8, 128), F32),
            pltpu.VMEM((1024, D), BF16),
            pltpu.VMEM((1024, D), BF16),
            pltpu.VMEM((events * 64, D), BF16),
            pltpu.VMEM((events * 64, D), BF16),
            pltpu.VMEM((2, 2, 4, 1, 128), jnp.int32),
            pltpu.VMEM((2, 4, 1, 128), jnp.int32),
            pltpu.VMEM((3, 8, 8, 128), F32),
            pltpu.VMEM((ROWS, D), F32),
            pltpu.VMEM((ROWS, 1), F32),
            pltpu.VMEM((ROWS, D), F32),
            pltpu.VMEM((ROWS, 1), F32),
            pltpu.VMEM((ROWS, D), BF16),
            pltpu.VMEM((ROWS, D), BF16),
            dma((2,)),
            dma((events,)), dma((events,)),
            dma((16,)), dma((16,)),
            dma((events,)), dma((events,)),
            dma((5,)), dma((5,)),
            dma((15,)), dma((15,)),
            dma((3, 7)), dma((3, 7)),
        ],
        compiler_params=pltpu.CompilerParams(
            collective_id=0, has_side_effects=True, vmem_limit_bytes=60 << 20
        ),
        cost_estimate=pl.CostEstimate(flops=3 * 2 * 2048 * 1024 * D, bytes_accessed=1 << 21, transcendentals=3 << 21),
        name="pair_loss",
    )(photo, sentence, photo_ids.reshape(1, ROWS), sentence_ids.reshape(1, ROWS), sharp, offset)


def solution(mesh):
    return jax.shard_map(
        on_device,
        mesh=mesh,
        in_specs=(
            P(("img", "txt"), None),
            P(("txt", "img"), None),
            P(("img", "txt")),
            P(("txt", "img")),
            P(),
            P(),
        ),
        out_specs=(P(("img", "txt"), None), P(("txt", "img"), None), P()),
        check_vma=False,
    )
```
